768 devices in a mesh: img: 8 (over x, z_hi), txt: 96 (over y, z_lo, core).
Axes of the slice: x: 4, y: 8, z: 12 (z_hi: 2, z_lo: 6; z = z_hi * 6 + z_lo), core: 2. Of those that a mesh axis runs over, the one named last changes fastest.
Arguments:
- picture_vectors: bfloat16 [12288, 768], P(('img', 'txt')), may hold values from -6 to 6
- caption_vectors: bfloat16 [12288, 768], P(('txt', 'img')), may hold values from -6 to 6
- heat_exponent: float32 [], replicated, may hold values from 1.4 to 2.8
- offset_shift: float32 [], replicated, may hold values from -6 to -3
Outputs:
- grad_image: float32 [12288, 768], P(('img', 'txt'))
- grad_text: float32 [12288, 768], P(('txt', 'img'))
- couple_means: float32 [3], replicated
The draws below stay inside these ranges and needn't reach their ends.
All inputs are finite; a program needn't handle non-finite values.
Results may differ from the reference program's by a relative error of at most 0.0033.
The reference program's roundings to bfloat16 on the way count: a program that leaves them out, or rounds other values in their place, can miss the bound.
Values may be sent and summed in bfloat16 or wider, within the bound.
A program may use at most 32 MiB of HBM per device.

```python
import jax
import jax.numpy as jnp
from jax import lax

E = 768
BATCH = 12288
N_IMG = 8


def block_scale(rng, shape, shards, low, high):
    loudness, own = 1.0, jax.random.fold_in(rng, 6)
    for axis_at, parts in shards:
        steps = jnp.exp(jax.random.uniform(jax.random.fold_in(own, axis_at), (parts,), jnp.float32, low / len(shards), high / len(shards)))
        loudness = loudness * jnp.repeat(steps, shape[axis_at] // parts).reshape([-1 if axis == axis_at else 1 for axis in range(len(shape))])
    return loudness


def scatter_about(own_key, extent, width, most, shards=(), kind=jnp.bfloat16):
    level = block_scale(own_key, extent, shards, -0.22, 0.18) if shards else 1.0
    result = jax.random.normal(own_key, extent, jnp.float32) * width * level
    return jnp.minimum(jnp.maximum(result, -most), most).astype(kind)


def setup_inputs(seed: int = 0) -> dict:
    keys = jax.random.split(jax.random.key(seed), 5)
    return {
        "picture_vectors": scatter_about(keys[0], (BATCH, E), 1.0, 6.0, ((0, 768),)),
        "caption_vectors": scatter_about(keys[1], (BATCH, E), 1.0, 6.0, ((0, 768),)),
        "heat_exponent": jnp.clip(jax.random.uniform(keys[2], (), jnp.float32, 1.4, 2.8), 1.4, 2.8),
        "offset_shift": jnp.clip(jax.random.uniform(keys[3], (), jnp.float32, -6.0, -3.0), -6.0, -3.0),
    }


epsilon = 1e-06

def normalize(raw):
    values = raw.astype(jnp.float32)
    norm_rows = jnp.sqrt(lax.optimization_barrier(jnp.sum(values * values, axis=1, keepdims=True)) + epsilon)
    return (values / norm_rows, norm_rows)

def back_norm(unit, direction, norm_rows):
    inner = lax.optimization_barrier(jnp.sum(unit * direction, axis=1, keepdims=True))
    return (direction - unit * inner) / norm_rows

def reference(picture_vectors, caption_vectors, heat_exponent, offset_shift):
    image_unit, image_norm = normalize(picture_vectors)
    text_unit, text_norm = normalize(caption_vectors)
    image_bf = image_unit.astype(jnp.bfloat16)
    text_bf = text_unit.astype(jnp.bfloat16)
    heat_factor = jnp.exp(heat_exponent)
    sample_number = image_bf.shape[0]
    block_rows = sample_number // N_IMG
    blocks = image_bf.reshape(N_IMG, block_rows, image_bf.shape[1])
    starts = jnp.arange(N_IMG, dtype=jnp.int32) * block_rows
    columns = jnp.arange(sample_number, dtype=jnp.int32)

    def one_block(carry, inputs):
        text_acc, loss_acc, coeff_acc, prod_acc = carry
        image_rows, start = inputs
        cosine_table = jnp.dot(image_rows, text_bf.T, preferred_element_type=jnp.float32)
        couple_scores = heat_factor * cosine_table + offset_shift
        row_ids = start + jnp.arange(block_rows, dtype=jnp.int32)
        label = jnp.where(row_ids[:, None] == columns[None, :], 1.0, -1.0).astype(jnp.float32)
        pair_loss = jax.nn.softplus(-label * couple_scores)
        couple_weight = -label * jax.nn.sigmoid(-label * couple_scores)
        stretched_cosines = (heat_factor * couple_weight).astype(jnp.bfloat16)
        image_dir = jnp.dot(stretched_cosines, text_bf, preferred_element_type=jnp.float32)
        text_acc = text_acc + jnp.dot(stretched_cosines.T, image_rows, preferred_element_type=jnp.float32)
        carry = (text_acc, loss_acc + jnp.sum(pair_loss), coeff_acc + jnp.sum(couple_weight), prod_acc + jnp.sum(couple_weight * cosine_table))
        return (carry, image_dir)
    start_carry = (jnp.zeros(text_bf.shape, jnp.float32), jnp.zeros((), jnp.float32), jnp.zeros((), jnp.float32), jnp.zeros((), jnp.float32))
    final, image_dirs = lax.scan(one_block, start_carry, (blocks, starts))
    text_dir, penalty_accumulated, weight_accumulated, multiplied_accumulated = final
    image_dir = image_dirs.reshape(image_bf.shape)
    grad_image = back_norm(image_unit, image_dir, image_norm)
    grad_text = back_norm(text_unit, text_dir, text_norm)
    couple_means = jnp.stack([penalty_accumulated, weight_accumulated, heat_factor * multiplied_accumulated]) / (float(sample_number) * float(sample_number))
    return (grad_image, grad_text, couple_means)
```

```python
import functools

import jax
import jax.numpy as jnp
from jax import lax
from jax.experimental import pallas as pl
from jax.experimental.pallas import tpu as pltpu
from jax.sharding import PartitionSpec as P

MESH = pl.DeviceIdType.MESH
NX, NY, NZ = 4, 8, 12
B, E = 16, 768
EPS = 1e-6
COUNT = 12288.0

DY = (0, 1, 7, 2, 6, 3, 5, 4)
GROUPS = ((0, 1), (1, 3), (3, 5), (5, 8))
NEAR = (0, 1, 11, 2)
IMG, TXT = NX * NY * B, NZ * 2 * B
XR, CR = NY * B, NZ * B


def kernel(
    pic, cap, heat, shift, g_img, g_txt, means,
    images, texts, sims, scaled, scaled_t, img_send, img_own, txt_send, txt_own,
    from_x, to_y, from_y, from_c, to_near, from_near, to_far, from_far, part, sum_in,
    s_gather, r_gather, s_scatter, r_scatter, s_sum, r_sum,
):
    img, txt = lax.axis_index("img"), lax.axis_index("txt")
    x, y, c = img // 2, txt // 12, txt % 2
    z = (img % 2) * 6 + (txt // 2) % 6
    way = 1 - 2 * c

    def at(dx=0, dy=0, dz=0, dc=0):
        zz = (z + way * dz + 2 * NZ) % NZ
        return (((x + dx + NX) % NX) * 2 + zz // 6,
                (((y + dy + NY) % NY) * 6 + zz % 6) * 2 + (c + dc) % 2)

    peers = [at(dx=d) for d in (1, 2, 3)] + [at(dy=d) for d in range(1, 8)]
    peers += [at(dz=d) for d in (1, 11, 2, 10, 4, 8)] + [at(dc=1)]
    entry = pltpu.get_barrier_semaphore()
    for peer in peers:
        pl.semaphore_signal(entry, inc=1, device_id=peer, device_id_type=MESH)

    def normalize(ref):
        values = ref[...].astype(jnp.float32)
        norm = jnp.sqrt(jnp.sum(values * values, axis=1, keepdims=True) + EPS)
        return values / norm, norm

    img_unit, img_norm = normalize(pic)
    txt_unit, txt_norm = normalize(cap)
    images[0:B, :] = img_unit.astype(jnp.bfloat16)
    texts[0:B, :] = txt_unit.astype(jnp.bfloat16)
    pl.semaphore_wait(entry, len(peers))

    sends = []

    def sender(ssem, rsem):
        used = [0]

        def send(src, dst, device):
            i = used[0]
            used[0] += 1
            copy = pltpu.make_async_remote_copy(
                src_ref=src, dst_ref=dst, send_sem=ssem.at[i], recv_sem=rsem.at[i],
                device_id=device, device_id_type=MESH)
            copy.start()
            sends.append(copy)
            return copy

        return send

    def rows(ref, first, count):
        return ref.at[pl.ds(first, count)]

    send = sender(s_gather, r_gather)
    own_t, own_i = rows(texts, 0, B), rows(images, 0, B)
    far = [send(own_t, rows(texts, f * B, B), at(dz=-4 * f)) for f in (1, 2)]
    over_y = {k: send(own_i, rows(images, k * B, B), at(dy=-DY[k])) for k in range(7, 0, -1)}
    arrive_x, arrive_z, arrive_c = [], [], []

    def forward_x(g):
        a, b = GROUPS[g]
        for dx in (2, 1, 3):
            arrive_x.append(send(rows(images, a * B, (b - a) * B),
                                 rows(images, dx * XR + a * B, (b - a) * B), at(dx=-dx)))

    forward_x(0)
    near = {n: [send(own_t, rows(texts, n * 3 * B, B), at(dz=-NEAR[n]))] for n in (3, 1, 2)}
    for g in (1, 2):
        for k in range(*GROUPS[g]):
            over_y[k].wait_recv()
        forward_x(g)
    for copy in far:
        copy.wait_recv()
    for n in (3, 1, 2):
        near[n].append(send(rows(texts, B, 2 * B), rows(texts, (n * 3 + 1) * B, 2 * B), at(dz=-NEAR[n])))
    arrive_c.append(send(rows(texts, 0, 3 * B), rows(texts, CR, 3 * B), at(dc=1)))
    for k in range(*GROUPS[3]):
        over_y[k].wait_recv()
    forward_x(3)
    for n in (1, 2, 3):
        for copy in near[n]:
            copy.wait_recv()
        arrive_c.append(send(rows(texts, n * 3 * B, 3 * B), rows(texts, CR + n * 3 * B, 3 * B), at(dc=1)))
    for copy in arrive_c + arrive_x:
        copy.wait_recv()

    nt = (((1,), (1,)), ((), ()))
    sims[...] = lax.dot_general(images[...], texts[...], nt, preferred_element_type=jnp.float32)

    slot = lax.broadcasted_iota(jnp.int32, (1, TXT), 1)
    row = slot & (B - 1)
    slot = slot >> 4
    dc = jnp.where(slot >= 12, 1, 0)
    slot = slot - 12 * dc
    n = jnp.where(slot >= 9, 3, jnp.where(slot >= 6, 2, jnp.where(slot >= 3, 1, 0)))
    f = slot - 3 * n
    dz = jnp.where(n == 2, 11, jnp.where(n == 3, 2, n)) + 4 * f
    dz = jnp.where(dz >= 12, dz - 12, dz)
    zz = z + way * (1 - 2 * dc) * dz
    zz = jnp.where(zz >= 12, zz - 12, jnp.where(zz < 0, zz + 12, zz))
    z_hi = jnp.where(zz >= 6, 1, 0)
    cc = c + dc - 2 * c * dc
    txt_id = (((y * 6 + zz - 6 * z_hi) * 2 + cc) * 8 + x * 2 + z_hi) * B + row

    temp = jnp.exp(jnp.full((1, TXT), heat[0], jnp.float32))
    bias = shift[0]
    step = 32

    def pairs(i, sums):
        first = pl.multiple_of(i * step, step)
        sim = sims[pl.ds(first, step), :]
        r = lax.broadcasted_iota(jnp.int32, (step, 1), 0) + first
        s = r >> 4
        k = s & 7
        dy = jnp.where((k & 1) == 1, (k + 1) >> 1, (8 - (k >> 1)) & 7)
        xo, yo = (x + (s >> 3)) & 3, (y + dy) & 7
        img_id = ((xo * 2 + z // 6) * 96 + (yo * 6 + z % 6) * 2 + c) * B + (r & (B - 1))
        same = img_id == txt_id
        logits = temp * sim + bias
        arg = jnp.where(same, -logits, logits)
        e = jnp.exp(-jnp.abs(arg))
        loss = jnp.maximum(arg, 0.0) + jnp.log1p(e)
        sig = jnp.where(arg >= 0, 1.0, e) / (1.0 + e)
        coeff = jnp.where(same, -sig, sig)
        scaled[pl.ds(first, step), :] = (temp * coeff).astype(jnp.bfloat16)

        def fold(v):
            return jnp.sum(v.reshape(step // 8, 8, TXT), axis=0)

        return sums[0] + fold(loss), sums[1] + fold(coeff), sums[2] + fold(coeff * sim)

    zero = jnp.zeros((8, TXT), jnp.float32)
    sums = lax.fori_loop(0, IMG // step, pairs, (zero, zero, zero))

    def lanes(v):
        v = v[:, 0:128] + v[:, 128:256] + v[:, 256:384]
        return jnp.sum(v, axis=0, keepdims=True)

    sub = lax.broadcasted_iota(jnp.int32, (8, 128), 0)
    total = jnp.where(sub == 0, lanes(sums[0]), 0.0) + jnp.where(sub == 1, lanes(sums[1]), 0.0)
    total = total + jnp.where(sub == 2, lanes(sums[2]), 0.0)

    send_sum = sender(s_sum, r_sum)
    used = [0]

    def spread(stage, devices):
        copies = []
        for device in devices:
            copies.append((send_sum(part.at[stage], sum_in.at[used[0]], device), used[0]))
            used[0] += 1
        return copies

    def collect(value, copies):
        for copy, i in copies:
            copy.wait_recv()
            value = value + sum_in[i]
        return value

    part[0] = total
    sum_c = spread(0, [at(dc=1)])

    send = sender(s_scatter, r_scatter)
    scaled_t[...] = scaled[...].T
    for half in (1, 0):
        term = jnp.dot(scaled_t[half * CR:(half + 1) * CR, :], images[...], preferred_element_type=jnp.float32)
        if half:
            txt_send[...] = term.astype(jnp.bfloat16)
            over_c = send(txt_send, from_c, at(dc=1))
        else:
            txt_own[...] = term
    for dx in (2, 1, 3, 0):
        term = jnp.dot(scaled[dx * XR:(dx + 1) * XR, :], texts[...], preferred_element_type=jnp.float32)
        if dx:
            img_send[(dx - 1) * XR:dx * XR, :] = term.astype(jnp.bfloat16)
        else:
            img_own[...] = term
    over_x = {}
    for g in (3, 2, 1, 0):
        a, b = GROUPS[g]
        for dx in (2, 1, 3):
            first = (dx - 1) * XR + a * B
            over_x[g, dx] = send(rows(img_send, first, (b - a) * B), rows(from_x, first, (b - a) * B), at(dx=dx))

    total = collect(total, sum_c)
    part[1] = total
    sum_f = spread(1, [at(dz=4), at(dz=8)])

    over_c.wait_recv()
    to_near[...] = (txt_own[3 * B:, :] + from_c[3 * B:, :].astype(jnp.float32)).astype(jnp.bfloat16)
    over_near = [send(rows(to_near, (n - 1) * 3 * B, 3 * B), rows(from_near, (n - 1) * 3 * B, 3 * B), at(dz=NEAR[n]))
                 for n in (3, 1, 2)]
    txt_three = txt_own[0:3 * B, :] + from_c[0:3 * B, :].astype(jnp.float32)

    over_y = []
    for g in (3, 2, 1, 0):
        a, b = GROUPS[g]
        mine = img_own[a * B:b * B, :]
        for dx in (2, 1, 3):
            over_x[g, dx].wait_recv()
        for dx in (1, 2, 3):
            mine = mine + from_x[(dx - 1) * XR + a * B:(dx - 1) * XR + b * B, :].astype(jnp.float32)
        if g:
            to_y[(a - 1) * B:(b - 1) * B, :] = mine.astype(jnp.bfloat16)
            for k in range(b - 1, a - 1, -1):
                over_y.append(send(rows(to_y, (k - 1) * B, B), rows(from_y, (k - 1) * B, B), at(dy=DY[k])))
        else:
            img_dir = mine
        if g == 3:
            total = collect(total, sum_f)
            part[2] = total
            sum_n = spread(2, [at(dz=NEAR[n]) for n in (3, 1, 2)])
        if g == 2:
            for copy in over_near:
                copy.wait_recv()
            for n in (1, 2, 3):
                txt_three = txt_three + from_near[(n - 1) * 3 * B:n * 3 * B, :].astype(jnp.float32)
            to_far[...] = txt_three[B:, :].astype(jnp.bfloat16)
            over_far = [send(rows(to_far, (f - 1) * B, B), rows(from_far, (f - 1) * B, B), at(dz=4 * f)) for f in (1, 2)]
            txt_dir = txt_three[0:B, :]
            total = collect(total, sum_n)
            part[3] = total
            sum_x = spread(3, [at(dx=d) for d in (2, 1, 3)])

    total = collect(total, sum_x)
    part[4] = total
    sum_y = spread(4, [at(dy=d) for d in DY[:0:-1]])

    def back_norm(unit, direction, norm):
        inner = jnp.sum(unit * direction, axis=1, keepdims=True)
        return (direction - unit * inner) / norm

    for copy in over_far:
        copy.wait_recv()
    for f in (1, 2):
        txt_dir = txt_dir + from_far[(f - 1) * B:f * B, :].astype(jnp.float32)
    g_txt[...] = back_norm(txt_unit, txt_dir, txt_norm)
    for copy in over_y:
        copy.wait_recv()
    for k in range(1, 8):
        img_dir = img_dir + from_y[(k - 1) * B:k * B, :].astype(jnp.float32)
    g_img[...] = back_norm(img_unit, img_dir, img_norm)
    total = collect(total, sum_y)
    scale = 1.0 / (COUNT * COUNT)
    means[0] = jnp.sum(jnp.where(sub == 0, total, 0.0)) * scale
    means[1] = jnp.sum(jnp.where(sub == 1, total, 0.0)) * scale
    means[2] = jnp.sum(jnp.where(sub == 2, total * temp[:, 0:128], 0.0)) * scale
    for copy in sends:
        copy.wait_send()


def per_device(pictures, captions, heat, shift):
    f32, bf16 = jnp.float32, jnp.bfloat16
    vmem, smem = pl.BlockSpec(memory_space=pltpu.VMEM), pl.BlockSpec(memory_space=pltpu.SMEM)
    dma = pltpu.SemaphoreType.DMA
    return pl.pallas_call(
        kernel,
        out_shape=(
            jax.ShapeDtypeStruct((B, E), f32),
            jax.ShapeDtypeStruct((B, E), f32),
            jax.ShapeDtypeStruct((3,), f32),
        ),
        in_specs=[vmem, vmem, smem, smem],
        out_specs=(vmem, vmem, smem),
        scratch_shapes=[
            pltpu.VMEM((IMG, E), bf16),
            pltpu.VMEM((TXT, E), bf16),
            pltpu.VMEM((IMG, TXT), f32),
            pltpu.VMEM((IMG, TXT), bf16),
            pltpu.VMEM((TXT, IMG), bf16),
            pltpu.VMEM((3 * XR, E), bf16),
            pltpu.VMEM((XR, E), f32),
            pltpu.VMEM((CR, E), bf16),
            pltpu.VMEM((CR, E), f32),
            pltpu.VMEM((3 * XR, E), bf16),
            pltpu.VMEM((7 * B, E), bf16),
            pltpu.VMEM((7 * B, E), bf16),
            pltpu.VMEM((CR, E), bf16),
            pltpu.VMEM((9 * B, E), bf16),
            pltpu.VMEM((9 * B, E), bf16),
            pltpu.VMEM((2 * B, E), bf16),
            pltpu.VMEM((2 * B, E), bf16),
            pltpu.VMEM((5, 8, 128), f32),
            pltpu.VMEM((16, 8, 128), f32),
            dma((31,)), dma((31,)), dma((25,)), dma((25,)), dma((16,)), dma((16,)),
        ],
        compiler_params=pltpu.CompilerParams(
            collective_id=0, has_side_effects=True, vmem_limit_bytes=48 * 1024 * 1024),
        cost_estimate=pl.CostEstimate(flops=910_000_000, bytes_accessed=150_000, transcendentals=600_000),
        name="pairs",
    )(pictures, captions, heat.reshape(1), shift.reshape(1))


def solution(mesh):
    in_specs = (P(("img", "txt"), None), P(("txt", "img"), None), P(), P())
    out_specs = (P(("img", "txt"), None), P(("txt", "img"), None), P())
    return jax.shard_map(
        per_device, mesh=mesh, in_specs=in_specs, out_specs=out_specs, check_vma=False
    )
```

```python
import jax
import jax.numpy as jnp
from jax import lax
from jax.experimental import pallas as pl
from jax.experimental.pallas import tpu as pltpu
from jax.sharding import PartitionSpec as P

MESH = pl.DeviceIdType.MESH
NX, NY, NZ = 4, 8, 12
B, E = 16, 768
EPS = 1e-6
COUNT = 12288.0
HALF = E // 2

DY = (0, 1, 7, 2, 6, 3, 5, 4)
DZ = (0, 1, 11, 2, 10, 3, 9, 4, 8, 5, 7, 6)
SLOT = {d: k for k, d in enumerate(DZ)}
IMG, TXT = NX * NY * B, NZ * 2 * B
CR = NZ * B
FIRST = 5 * NX * B
PARTS = ((0, FIRST), (FIRST, IMG))
DX = (2, 1, 3)


def kernel(
    pic_in, cap_in, heat, shift, g_img, g_txt, means,
    pic, cap, images, texts, sims, scaled, scaled_t, img_term, img_send, txt_send, txt_own,
    from_x, to_y, from_y, from_c, to_z, from_z, to_far, part, sum_in,
    s_in, s_gather, r_gather, s_scatter, r_scatter, s_sum, r_sum,
):
    img, txt = lax.axis_index("img"), lax.axis_index("txt")
    x, y, c = img // 2, txt // 12, txt % 2
    z = (img % 2) * 6 + (txt // 2) % 6

    def at(dx=0, dy=0, dz=0, dc=0):
        zz = (z + dz) % NZ
        return (((x + dx) % NX) * 2 + zz // 6, (((y + dy) % NY) * 6 + zz % 6) * 2 + (c + dc) % 2)

    peers = [at(dy=d) for d in (4, 3, 5, 2, 6, 1, 7)] + [at(dx=d) for d in DX]
    peers += [at(dz=d) for d in (4, 8, 3, 9, 2, 10, 1, 11)] + [at(dc=1)]
    entry = pltpu.get_barrier_semaphore()
    for peer in peers:
        pl.semaphore_signal(entry, inc=1, device_id=peer, device_id_type=MESH)
    loads = [pltpu.make_async_copy(pic_in, pic, s_in.at[0]), pltpu.make_async_copy(cap_in, cap, s_in.at[1])]
    for load in loads:
        load.start()
    for load in loads:
        load.wait()

    def normalize(ref):
        values = ref[...].astype(jnp.float32)
        norm = jnp.sqrt(jnp.sum(values * values, axis=1, keepdims=True) + EPS)
        return values / norm, norm

    img_unit, img_norm = normalize(pic)
    txt_unit, txt_norm = normalize(cap)
    images[0:B, :] = img_unit.astype(jnp.bfloat16)
    texts[0:B, :] = txt_unit.astype(jnp.bfloat16)
    pl.semaphore_wait(entry, len(peers))

    sends = []

    def sender(ssem, rsem):
        used = [0]

        def send(src, dst, device):
            i = used[0]
            used[0] += 1
            copy = pltpu.make_async_remote_copy(
                src_ref=src, dst_ref=dst, send_sem=ssem.at[i], recv_sem=rsem.at[i],
                device_id=device, device_id_type=MESH)
            copy.start()
            sends.append(copy)
            return copy

        return send

    def slots(ref, first, count=1):
        return ref.at[pl.ds(first * B, count * B)]

    def wait(copies):
        for copy in copies:
            copy.wait_recv()

    send = sender(s_gather, r_gather)
    own_t, own_i = slots(texts, 0), slots(images, 0)
    over_z = {d: send(own_t, slots(texts, SLOT[d]), at(dz=-d)) for d in (4, 8, 3, 9, 2, 10, 1, 11)}
    over_y = {k: send(own_i, slots(images, 4 * k), at(dy=-DY[k])) for k in range(1, 8)}
    over_x, over_c = {}, []

    def forward_x(*ks):
        for k in ks:
            if k:
                over_y[k].wait_recv()
            over_x[k] = [send(slots(images, 4 * k), slots(images, 4 * k + dx), at(dx=-dx)) for dx in DX]

    def forward_c(*ds):
        first = min(SLOT[d] for d in ds)
        over_c.append(send(slots(texts, first, len(ds)), slots(texts, NZ + first, len(ds)), at(dc=1)))

    forward_x(0)
    forward_c(0)
    wait([over_z[4], over_z[8]])
    six = SLOT[6] * B
    late = [
        send(texts.at[pl.ds(SLOT[4] * B, B), pl.ds(0, HALF)], texts.at[pl.ds(six, B), pl.ds(0, HALF)], at(dz=-2)),
        send(texts.at[pl.ds(SLOT[8] * B, B), pl.ds(HALF, HALF)], texts.at[pl.ds(six, B), pl.ds(HALF, HALF)], at(dz=2)),
        send(slots(texts, SLOT[4]), slots(texts, SLOT[5]), at(dz=-1)),
        send(slots(texts, SLOT[8]), slots(texts, SLOT[7]), at(dz=1)),
    ]
    forward_x(1, 2, 3, 4)
    forward_c(4, 8)
    wait([over_z[d] for d in (1, 11, 2, 10)])
    forward_c(1, 11, 2, 10)
    forward_x(5, 6, 7)
    wait([over_z[d] for d in (3, 9)])
    forward_c(3, 9)
    wait(late)
    forward_c(5, 7, 6)

    def owner_offset(k, n):
        return jnp.where((k & 1) == 1, (k + 1) >> 1, jnp.where(k == 0, 0, n - (k >> 1)))

    col = lax.broadcasted_iota(jnp.int32, (1, TXT), 1)
    k = col >> 4
    dc = jnp.where(k >= NZ, 1, 0)
    zz = z + owner_offset(k - NZ * dc, NZ)
    zz = jnp.where(zz >= NZ, zz - NZ, zz)
    z_hi = jnp.where(zz >= 6, 1, 0)
    cc = c + dc - 2 * c * dc
    txt_id = (((y * 6 + zz - 6 * z_hi) * 2 + cc) * 8 + x * 2 + z_hi) * B + (col & (B - 1))
    temp = jnp.exp(jnp.full((1, TXT), heat[0], jnp.float32))
    bias = shift[0]
    step = 32

    def pairs(i, sums):
        first = pl.multiple_of(i * step, step)
        sim = sims[pl.ds(first, step), :]
        r = lax.broadcasted_iota(jnp.int32, (step, 1), 0) + first
        xo = (x + (r >> 4)) & (NX - 1)
        yo = (y + owner_offset(r >> 6, NY)) & (NY - 1)
        img_id = ((xo * 2 + z // 6) * 96 + (yo * 6 + z % 6) * 2 + c) * B + (r & (B - 1))
        same = img_id == txt_id
        logits = temp * sim + bias
        arg = jnp.where(same, -logits, logits)
        e = jnp.exp(-jnp.abs(arg))
        loss = jnp.maximum(arg, 0.0) + jnp.log1p(e)
        sig = jnp.where(arg >= 0, 1.0, e) / (1.0 + e)
        coeff = jnp.where(same, -sig, sig)
        scaled[pl.ds(first, step), :] = (temp * coeff).astype(jnp.bfloat16)

        def fold(v):
            return jnp.sum(v.reshape(step // 8, 8, TXT), axis=0)

        return sums[0] + fold(loss), sums[1] + fold(coeff), sums[2] + fold(coeff * sim)

    zero = jnp.zeros((8, TXT), jnp.float32)
    sums = (zero, zero, zero)
    send = sender(s_scatter, r_scatter)
    nt = (((1,), (1,)), ((), ()))
    back_x = {}
    wait(over_c)
    for p, (a, b) in enumerate(PARTS):
        ks = (range(0, 5), range(5, 8))[p]
        for k in ks:
            wait(over_x[k])
        sims[a:b, :] = lax.dot_general(images[a:b, :], texts[...], nt, preferred_element_type=jnp.float32)
        sums = lax.fori_loop(a // step, b // step, pairs, sums)
        if p:
            def whole(v):
                v = v[:, 0:128] + v[:, 128:256] + v[:, 256:384]
                return jnp.sum(jnp.sum(v, axis=0, keepdims=True), axis=1, keepdims=True)

            lane = lax.broadcasted_iota(jnp.int32, (1, 128), 1)
            total = jnp.where(lane == 0, whole(sums[0]), jnp.where(lane == 1, whole(sums[1]), whole(sums[2])))
            send_sum = sender(s_sum, r_sum)
            used = [0]

            def spread(stage, value, devices):
                part[stage] = value
                copies = []
                for device in devices:
                    copies.append((send_sum(part.at[stage], sum_in.at[used[0]], device), used[0]))
                    used[0] += 1
                return copies

            def collect(value, copies):
                for copy, i in copies:
                    copy.wait_recv()
                    value = value + sum_in[i]
                return value

            sum_c = spread(0, total, [at(dc=1)])
        term = jnp.dot(scaled[a:b, :], texts[...], preferred_element_type=jnp.float32)
        img_term[a:b, :] = term
        img_send[a:b, :] = term.astype(jnp.bfloat16)
    def send_x(*ks):
        for k in ks:
            back_x[k] = [send(slots(img_send, 4 * k + dx), slots(from_x, 4 * k + dx), at(dx=dx)) for dx in DX]

    send_x(7, 6, 5)
    scaled_t[...] = scaled[...].T
    txt_send[...] = jnp.dot(scaled_t[CR:, :], images[...], preferred_element_type=jnp.float32).astype(jnp.bfloat16)
    back_c = send(txt_send, from_c, at(dc=1))
    txt_own[...] = jnp.dot(scaled_t[0:CR, :], images[...], preferred_element_type=jnp.float32)
    total = collect(total, sum_c)
    plane = [at(dx, dy) for dy in DY[::-1] for dx in (2, 1, 3, 0) if dx or dy]
    sum_p = spread(1, total, plane)

    back_c.wait_recv()
    txt_own[...] = txt_own[...] + from_c[...].astype(jnp.float32)
    to_z[...] = txt_own[...].astype(jnp.bfloat16)
    relay = [
        send(to_z.at[pl.ds(six, B), pl.ds(0, HALF)], from_z.at[pl.ds(six, B), pl.ds(0, HALF)], at(dz=2)),
        send(to_z.at[pl.ds(six, B), pl.ds(HALF, HALF)], from_z.at[pl.ds(six, B), pl.ds(HALF, HALF)], at(dz=-2)),
        send(slots(to_z, SLOT[5]), slots(from_z, SLOT[5]), at(dz=1)),
        send(slots(to_z, SLOT[7]), slots(from_z, SLOT[7]), at(dz=-1)),
    ]
    back_z = {d: send(slots(to_z, SLOT[d]), slots(from_z, SLOT[d]), at(dz=d)) for d in (3, 9, 2, 10, 1, 11)}
    for k in (7, 6, 5):
        for copy in back_x[k]:
            copy.wait_send()
    send_x(4, 3, 2, 1, 0)

    wait(relay)

    def piece(ref, d):
        return ref[SLOT[d] * B:(SLOT[d] + 1) * B, :].astype(jnp.float32)

    side = lax.broadcasted_iota(jnp.int32, (B, E), 1) < HALF
    both = piece(from_z, 6)
    to_far[0:B, :] = (piece(txt_own, 4) + piece(from_z, 5) + jnp.where(side, both, 0.0)).astype(jnp.bfloat16)
    to_far[B:, :] = (piece(txt_own, 8) + piece(from_z, 7) + jnp.where(side, 0.0, both)).astype(jnp.bfloat16)
    for i, d in enumerate((4, 8)):
        back_z[d] = send(slots(to_far, i), slots(from_z, SLOT[d]), at(dz=d))
    back_y = []

    def image_sum(k):
        wait(back_x[k])
        first = 4 * k * B
        value = img_term[first:first + B, :]
        for dx in (1, 2, 3):
            value = value + from_x[first + dx * B:first + (dx + 1) * B, :].astype(jnp.float32)
        return value

    def send_y(*ks):
        for k in ks:
            to_y[(k - 1) * B:k * B, :] = image_sum(k).astype(jnp.bfloat16)
            back_y.append(send(slots(to_y, k - 1), slots(from_y, k - 1), at(dy=DY[k])))

    total = collect(total, sum_p)
    sum_z = spread(2, total, [at(dz=d) for d in DZ[:0:-1]])
    send_y(7, 6, 5)
    send_y(4, 3, 2, 1)
    img_dir = image_sum(0)

    def back_norm(unit, direction, norm):
        inner = jnp.sum(unit * direction, axis=1, keepdims=True)
        return (direction - unit * inner) / norm

    txt_dir = piece(txt_own, 0)
    for d in (1, 11, 2, 10, 3, 9, 4, 8):
        back_z[d].wait_recv()
        txt_dir = txt_dir + piece(from_z, d)
    g_txt[...] = back_norm(txt_unit, txt_dir, txt_norm)
    wait(back_y)
    for k in range(1, 8):
        img_dir = img_dir + from_y[(k - 1) * B:k * B, :].astype(jnp.float32)
    g_img[...] = back_norm(img_unit, img_dir, img_norm)
    total = collect(total, sum_z)
    means[...] = total * jnp.where(lane == 2, temp[:, 0:128], 1.0) * (1.0 / (COUNT * COUNT))
    early = {id(copy) for k in (7, 6, 5) for copy in back_x[k]}
    for copy in sends:
        if id(copy) not in early:
            copy.wait_send()


def hand_over(a, b, c, a_out, b_out, c_out):
    a_out[...] = a[...]
    b_out[...] = b[...]
    for i in range(3):
        c_out[i] = jnp.sum(c[:, i:i + 1])


def per_device(pictures, captions, heat, shift):
    f32, bf16 = jnp.float32, jnp.bfloat16
    hbm, vmem, smem = (pl.BlockSpec(memory_space=m) for m in (pltpu.HBM, pltpu.VMEM, pltpu.SMEM))
    dma = pltpu.SemaphoreType.DMA
    results_shape = (
        jax.ShapeDtypeStruct((B, E), f32),
        jax.ShapeDtypeStruct((B, E), f32),
        jax.ShapeDtypeStruct((1, 128), f32),
    )
    results = pl.pallas_call(
        kernel,
        out_shape=results_shape,
        in_specs=[hbm, hbm, smem, smem],
        out_specs=(vmem, vmem, vmem),
        scratch_shapes=[
            pltpu.VMEM((B, E), bf16),
            pltpu.VMEM((B, E), bf16),
            pltpu.VMEM((IMG, E), bf16),
            pltpu.VMEM((TXT, E), bf16),
            pltpu.VMEM((IMG, TXT), f32),
            pltpu.VMEM((IMG, TXT), bf16),
            pltpu.VMEM((TXT, IMG), bf16),
            pltpu.VMEM((IMG, E), f32),
            pltpu.VMEM((IMG, E), bf16),
            pltpu.VMEM((CR, E), bf16),
            pltpu.VMEM((CR, E), f32),
            pltpu.VMEM((IMG, E), bf16),
            pltpu.VMEM((7 * B, E), bf16),
            pltpu.VMEM((7 * B, E), bf16),
            pltpu.VMEM((CR, E), bf16),
            pltpu.VMEM((CR, E), bf16),
            pltpu.VMEM((CR, E), bf16),
            pltpu.VMEM((2 * B, E), bf16),
            pltpu.VMEM((3, 1, 128), f32),
            pltpu.VMEM((43, 1, 128), f32),
            dma((2,)), dma((48,)), dma((48,)), dma((44,)), dma((44,)), dma((43,)), dma((43,)),
        ],
        compiler_params=pltpu.CompilerParams(
            collective_id=0, has_side_effects=True, vmem_limit_bytes=62 * 1024 * 1024),
        cost_estimate=pl.CostEstimate(flops=910_000_000, bytes_accessed=150_000, transcendentals=600_000),
        name="pairs",
    )(pictures, captions, heat.reshape(1), shift.reshape(1))
    return pl.pallas_call(
        hand_over,
        out_shape=(*results_shape[:2], jax.ShapeDtypeStruct((3,), f32)),
        in_specs=[vmem] * 3,
        out_specs=(vmem, vmem, smem),
        compiler_params=pltpu.CompilerParams(vmem_limit_bytes=62 * 1024 * 1024),
        name="hand_over",
    )(*results)


def solution(mesh):
    in_specs = (P(("img", "txt"), None), P(("txt", "img"), None), P(), P())
    out_specs = (P(("img", "txt"), None), P(("txt", "img"), None), P())
    return jax.shard_map(
        per_device, mesh=mesh, in_specs=in_specs, out_specs=out_specs, check_vma=False
    )
```

```python
import jax
import jax.numpy as jnp
from jax import lax
from jax.experimental import pallas as pl
from jax.experimental.pallas import tpu as pltpu
from jax.sharding import PartitionSpec as P

MESH = pl.DeviceIdType.MESH
NX, NY, NZ = 4, 8, 12
B, E = 16, 768
EPS = 1e-6
COUNT = 12288.0
HALF = E // 2

DY = (0, 1, 7, 2, 6, 3, 5, 4)
DZ = (0, 1, 11, 2, 10, 3, 9, 4, 8, 5, 7, 6)
SLOT = {d: k for k, d in enumerate(DZ)}
IMG, TXT = NX * NY * B, NZ * 2 * B
CR = NZ * B
FIRST = 5 * NX * B
PARTS = ((0, FIRST), (FIRST, IMG))
DX = (2, 1, 3)


def kernel(
    pic_in, cap_in, heat, shift, g_img, g_txt, means,
    pic, cap, images, texts, sims, scaled, scaled_t, img_term, img_send, txt_send, txt_own,
    from_x, to_y, from_y, from_y4, from_c, to_z, from_z, to_far, part, sum_in,
    s_in, s_gather, r_gather, s_scatter, r_scatter, s_sum, r_sum,
):
    img, txt = lax.axis_index("img"), lax.axis_index("txt")
    x, y, c = img // 2, txt // 12, txt % 2
    z = (img % 2) * 6 + (txt // 2) % 6

    def at(dx=0, dy=0, dz=0, dc=0):
        zz = (z + dz) % NZ
        return (((x + dx) % NX) * 2 + zz // 6, (((y + dy) % NY) * 6 + zz % 6) * 2 + (c + dc) % 2)

    peers = [at(dy=d) for d in (4, 3, 5, 2, 6, 1, 7)] + [at(dx=d) for d in DX]
    peers += [at(dz=d) for d in (4, 8, 3, 9, 2, 10, 1, 11)] + [at(dc=1)]
    entry = pltpu.get_barrier_semaphore()
    for peer in peers:
        pl.semaphore_signal(entry, inc=1, device_id=peer, device_id_type=MESH)
    loads = [pltpu.make_async_copy(pic_in, pic, s_in.at[0]), pltpu.make_async_copy(cap_in, cap, s_in.at[1])]
    for load in loads:
        load.start()
    for load in loads:
        load.wait()

    def normalize(ref):
        values = ref[...].astype(jnp.float32)
        norm = jnp.sqrt(jnp.sum(values * values, axis=1, keepdims=True) + EPS)
        return values / norm, norm

    img_unit, img_norm = normalize(pic)
    txt_unit, txt_norm = normalize(cap)
    images[0:B, :] = img_unit.astype(jnp.bfloat16)
    texts[0:B, :] = txt_unit.astype(jnp.bfloat16)
    pl.semaphore_wait(entry, len(peers))

    sends = []

    def sender(ssem, rsem):
        used = [0]

        def send(src, dst, device):
            i = used[0]
            used[0] += 1
            copy = pltpu.make_async_remote_copy(
                src_ref=src, dst_ref=dst, send_sem=ssem.at[i], recv_sem=rsem.at[i],
                device_id=device, device_id_type=MESH)
            copy.start()
            sends.append(copy)
            return copy

        return send

    def slots(ref, first, count=1):
        return ref.at[pl.ds(first * B, count * B)]

    def wait(copies):
        for copy in copies:
            copy.wait_recv()

    send = sender(s_gather, r_gather)
    own_t, own_i = slots(texts, 0), slots(images, 0)
    over_z = {d: send(own_t, slots(texts, SLOT[d]), at(dz=-d)) for d in (4, 8)}
    over_y = {k: send(own_i, slots(images, 4 * k), at(dy=-DY[k])) for k in range(1, 7)}
    over_x, over_c = {}, []

    def forward_x(*ks):
        for k in ks:
            if k:
                over_y[k].wait_recv()
            over_x[k] = [send(slots(images, 4 * k), slots(images, 4 * k + dx), at(dx=-dx)) for dx in DX]

    def forward_c(*ds):
        first = min(SLOT[d] for d in ds)
        over_c.append(send(slots(texts, first, len(ds)), slots(texts, NZ + first, len(ds)), at(dc=1)))

    forward_x(0)
    forward_c(0)
    forward_x(1, 2)
    for d in (3, 9, 2, 10, 1, 11):
        over_z[d] = send(own_t, slots(texts, SLOT[d]), at(dz=-d))
    wait(over_x[0])
    over_x[7] = [send(slots(images, 0, 4), slots(images, 28, 4), at(dy=-4))]
    wait([over_z[4], over_z[8]])
    six = SLOT[6] * B
    late = [
        send(texts.at[pl.ds(SLOT[4] * B, B), pl.ds(0, HALF)], texts.at[pl.ds(six, B), pl.ds(0, HALF)], at(dz=-2)),
        send(texts.at[pl.ds(SLOT[8] * B, B), pl.ds(HALF, HALF)], texts.at[pl.ds(six, B), pl.ds(HALF, HALF)], at(dz=2)),
        send(slots(texts, SLOT[4]), slots(texts, SLOT[5]), at(dz=-1)),
        send(slots(texts, SLOT[8]), slots(texts, SLOT[7]), at(dz=1)),
    ]
    forward_x(3, 4)
    forward_c(4, 8)
    wait([over_z[d] for d in (1, 11, 2, 10)])
    forward_c(1, 11, 2, 10)
    forward_x(5, 6)
    wait([over_z[d] for d in (3, 9)])
    forward_c(3, 9)
    wait(late)
    forward_c(5, 7, 6)

    def owner_offset(k, n):
        return jnp.where((k & 1) == 1, (k + 1) >> 1, jnp.where(k == 0, 0, n - (k >> 1)))

    col = lax.broadcasted_iota(jnp.int32, (1, TXT), 1)
    k = col >> 4
    dc = jnp.where(k >= NZ, 1, 0)
    zz = z + owner_offset(k - NZ * dc, NZ)
    zz = jnp.where(zz >= NZ, zz - NZ, zz)
    z_hi = jnp.where(zz >= 6, 1, 0)
    cc = c + dc - 2 * c * dc
    txt_id = (((y * 6 + zz - 6 * z_hi) * 2 + cc) * 8 + x * 2 + z_hi) * B + (col & (B - 1))
    temp = jnp.exp(jnp.full((1, TXT), heat[0], jnp.float32))
    bias = shift[0]
    step = 32

    def pairs(i, sums):
        first = pl.multiple_of(i * step, step)
        sim = sims[pl.ds(first, step), :]
        r = lax.broadcasted_iota(jnp.int32, (step, 1), 0) + first
        xo = (x + (r >> 4)) & (NX - 1)
        yo = (y + owner_offset(r >> 6, NY)) & (NY - 1)
        img_id = ((xo * 2 + z // 6) * 96 + (yo * 6 + z % 6) * 2 + c) * B + (r & (B - 1))
        same = img_id == txt_id
        logits = temp * sim + bias
        arg = jnp.where(same, -logits, logits)
        e = jnp.exp(-jnp.abs(arg))
        loss = jnp.maximum(arg, 0.0) + jnp.log1p(e)
        sig = jnp.where(arg >= 0, 1.0, e) / (1.0 + e)
        coeff = jnp.where(same, -sig, sig)
        scaled[pl.ds(first, step), :] = (temp * coeff).astype(jnp.bfloat16)

        def fold(v):
            return jnp.sum(v.reshape(step // 8, 8, TXT), axis=0)

        return sums[0] + fold(loss), sums[1] + fold(coeff), sums[2] + fold(coeff * sim)

    zero = jnp.zeros((8, TXT), jnp.float32)
    sums = (zero, zero, zero)
    send = sender(s_scatter, r_scatter)
    nt = (((1,), (1,)), ((), ()))
    back_x = {}
    wait(over_c)
    for p, (a, b) in enumerate(PARTS):
        ks = (range(0, 5), range(5, 8))[p]
        for k in ks:
            if k:
                wait(over_x[k])
        sims[a:b, :] = lax.dot_general(images[a:b, :], texts[...], nt, preferred_element_type=jnp.float32)
        sums = lax.fori_loop(a // step, b // step, pairs, sums)
        if p:
            def whole(v):
                v = v[:, 0:128] + v[:, 128:256] + v[:, 256:384]
                return jnp.sum(jnp.sum(v, axis=0, keepdims=True), axis=1, keepdims=True)

            lane = lax.broadcasted_iota(jnp.int32, (1, 128), 1)
            total = jnp.where(lane == 0, whole(sums[0]), jnp.where(lane == 1, whole(sums[1]), whole(sums[2])))
            send_sum = sender(s_sum, r_sum)
            used = [0]

            def spread(stage, value, devices):
                part[stage] = value
                copies = []
                for device in devices:
                    copies.append((send_sum(part.at[stage], sum_in.at[used[0]], device), used[0]))
                    used[0] += 1
                return copies

            def collect(value, copies):
                for copy, i in copies:
                    copy.wait_recv()
                    value = value + sum_in[i]
                return value

            plane = [at(dx, dy) for dy in DY[::-1] for dx in (2, 1, 3, 0) if dx or dy]
            sum_p = spread(0, total, plane)
            scaled_t[...] = scaled[...].T
            txt_send[...] = jnp.dot(scaled_t[CR:, :], images[...], preferred_element_type=jnp.float32).astype(jnp.bfloat16)
            cut = SLOT[4]
            back_c = [send(slots(txt_send, i, n), slots(from_c, i, n), at(dc=1)) for i, n in ((cut, NZ - cut), (0, cut))]
            txt_own[...] = jnp.dot(scaled_t[0:CR, :], images[...], preferred_element_type=jnp.float32)
        term = jnp.dot(scaled[a:b, :], texts[...], preferred_element_type=jnp.float32)
        img_term[a:b, :] = term
        img_send[a:b, :] = term.astype(jnp.bfloat16)
    def send_x(*ks):
        for k in ks:
            back_x[k] = [send(slots(img_send, 4 * k + dx), slots(from_x, 4 * k + dx), at(dx=dx)) for dx in DX]

    back_y4 = send(slots(img_send, 28, 4), from_y4, at(dy=4))
    send_x(6, 5, 4, 3, 2, 1)

    def add_c(first, last):
        value = txt_own[first * B:last * B, :] + from_c[first * B:last * B, :].astype(jnp.float32)
        txt_own[first * B:last * B, :] = value
        to_z[first * B:last * B, :] = value.astype(jnp.bfloat16)

    back_c[0].wait_recv()
    add_c(cut, NZ)
    relay = [
        send(to_z.at[pl.ds(six, B), pl.ds(0, HALF)], from_z.at[pl.ds(six, B), pl.ds(0, HALF)], at(dz=2)),
        send(to_z.at[pl.ds(six, B), pl.ds(HALF, HALF)], from_z.at[pl.ds(six, B), pl.ds(HALF, HALF)], at(dz=-2)),
        send(slots(to_z, SLOT[5]), slots(from_z, SLOT[5]), at(dz=1)),
        send(slots(to_z, SLOT[7]), slots(from_z, SLOT[7]), at(dz=-1)),
    ]
    back_c[1].wait_recv()
    add_c(0, cut)
    back_z = {}

    def send_z(*ds):
        for d in ds:
            back_z[d] = send(slots(to_z, SLOT[d]), slots(from_z, SLOT[d]), at(dz=d))

    send_z(2, 10, 1, 11)

    wait(relay)

    def piece(ref, d):
        return ref[SLOT[d] * B:(SLOT[d] + 1) * B, :].astype(jnp.float32)

    side = lax.broadcasted_iota(jnp.int32, (B, E), 1) < HALF
    both = piece(from_z, 6)
    to_far[0:B, :] = (piece(txt_own, 4) + piece(from_z, 5) + jnp.where(side, both, 0.0)).astype(jnp.bfloat16)
    to_far[B:, :] = (piece(txt_own, 8) + piece(from_z, 7) + jnp.where(side, 0.0, both)).astype(jnp.bfloat16)
    for i, d in enumerate((4, 8)):
        back_z[d] = send(slots(to_far, i), slots(from_z, SLOT[d]), at(dz=d))
    send_z(3, 9)
    total = collect(total, sum_p)
    column = [at(dz=d, dc=other) for d in DZ[::-1] for other in (0, 1) if d or other]
    sum_z = spread(1, total, column)
    back_y4.wait_recv()
    near_y = img_term[0:4 * B, :] + from_y4[...].astype(jnp.float32)
    img_term[0:4 * B, :] = near_y
    img_send[0:4 * B, :] = near_y.astype(jnp.bfloat16)
    send_x(0)
    back_y = []

    def image_sum(k):
        wait(back_x[k])
        first = 4 * k * B
        value = img_term[first:first + B, :]
        for dx in (1, 2, 3):
            value = value + from_x[first + dx * B:first + (dx + 1) * B, :].astype(jnp.float32)
        return value

    def send_y(*ks):
        for k in ks:
            to_y[(k - 1) * B:k * B, :] = image_sum(k).astype(jnp.bfloat16)
            back_y.append(send(slots(to_y, k - 1), slots(from_y, k - 1), at(dy=DY[k])))

    send_y(6, 5, 4, 3, 2, 1)
    img_dir = image_sum(0)

    def back_norm(unit, direction, norm):
        inner = jnp.sum(unit * direction, axis=1, keepdims=True)
        return (direction - unit * inner) / norm

    txt_dir = piece(txt_own, 0)
    for d in (1, 11, 2, 10, 3, 9, 4, 8):
        back_z[d].wait_recv()
        txt_dir = txt_dir + piece(from_z, d)
    g_txt[...] = back_norm(txt_unit, txt_dir, txt_norm)
    wait(back_y)
    for k in range(1, 7):
        img_dir = img_dir + from_y[(k - 1) * B:k * B, :].astype(jnp.float32)
    g_img[...] = back_norm(img_unit, img_dir, img_norm)
    total = collect(total, sum_z)
    means[...] = total * jnp.where(lane == 2, temp[:, 0:128], 1.0) * (1.0 / (COUNT * COUNT))
    for copy in sends:
        copy.wait_send()


def hand_over(a, b, c, a_out, b_out, c_out):
    a_out[...] = a[...]
    b_out[...] = b[...]
    for i in range(3):
        c_out[i] = jnp.sum(c[:, i:i + 1])


def per_device(pictures, captions, heat, shift):
    f32, bf16 = jnp.float32, jnp.bfloat16
    hbm, vmem, smem = (pl.BlockSpec(memory_space=m) for m in (pltpu.HBM, pltpu.VMEM, pltpu.SMEM))
    dma = pltpu.SemaphoreType.DMA
    results_shape = (
        jax.ShapeDtypeStruct((B, E), f32),
        jax.ShapeDtypeStruct((B, E), f32),
        jax.ShapeDtypeStruct((1, 128), f32),
    )
    results = pl.pallas_call(
        kernel,
        out_shape=results_shape,
        in_specs=[hbm, hbm, smem, smem],
        out_specs=(vmem, vmem, vmem),
        scratch_shapes=[
            pltpu.VMEM((B, E), bf16),
            pltpu.VMEM((B, E), bf16),
            pltpu.VMEM((IMG, E), bf16),
            pltpu.VMEM((TXT, E), bf16),
            pltpu.VMEM((IMG, TXT), f32),
            pltpu.VMEM((IMG, TXT), bf16),
            pltpu.VMEM((TXT, IMG), bf16),
            pltpu.VMEM((IMG, E), f32),
            pltpu.VMEM((IMG, E), bf16),
            pltpu.VMEM((CR, E), bf16),
            pltpu.VMEM((CR, E), f32),
            pltpu.VMEM((IMG, E), bf16),
            pltpu.VMEM((7 * B, E), bf16),
            pltpu.VMEM((7 * B, E), bf16),
            pltpu.VMEM((4 * B, E), bf16),
            pltpu.VMEM((CR, E), bf16),
            pltpu.VMEM((CR, E), bf16),
            pltpu.VMEM((CR, E), bf16),
            pltpu.VMEM((2 * B, E), bf16),
            pltpu.VMEM((2, 1, 128), f32),
            pltpu.VMEM((54, 1, 128), f32),
            dma((2,)), dma((48,)), dma((48,)), dma((44,)), dma((44,)), dma((54,)), dma((54,)),
        ],
        compiler_params=pltpu.CompilerParams(
            collective_id=0, has_side_effects=True, vmem_limit_bytes=62 * 1024 * 1024),
        cost_estimate=pl.CostEstimate(flops=910_000_000, bytes_accessed=150_000, transcendentals=600_000),
        name="pairs",
    )(pictures, captions, heat.reshape(1), shift.reshape(1))
    return pl.pallas_call(
        hand_over,
        out_shape=(*results_shape[:2], jax.ShapeDtypeStruct((3,), f32)),
        in_specs=[vmem] * 3,
        out_specs=(vmem, vmem, smem),
        compiler_params=pltpu.CompilerParams(vmem_limit_bytes=62 * 1024 * 1024),
        name="hand_over",
    )(*results)


def solution(mesh):
    in_specs = (P(("img", "txt"), None), P(("txt", "img"), None), P(), P())
    out_specs = (P(("img", "txt"), None), P(("txt", "img"), None), P())
    return jax.shard_map(
        per_device, mesh=mesh, in_specs=in_specs, out_specs=out_specs, check_vma=False
    )
```

```python
import jax
import jax.numpy as jnp
from jax import lax
from jax.experimental import pallas as pl
from jax.experimental.pallas import tpu as pltpu
from jax.sharding import PartitionSpec as P

MESH = pl.DeviceIdType.MESH
NX, NY, NZ = 4, 8, 12
B, E = 16, 768
EPS = 1e-6
COUNT = 12288.0
HALF = E // 2

DY = (0, 1, 7, 2, 6, 3, 5, 4)
DZ = (0, 1, 11, 2, 10, 3, 9, 4, 8, 5, 7, 6)
SLOT = {d: k for k, d in enumerate(DZ)}
IMG, TXT = NX * NY * B, NZ * 2 * B
CR = NZ * B
FIRST = 5 * NX * B
PARTS = ((0, FIRST), (FIRST, IMG))
DX = (2, 1, 3)


def kernel(
    pic_in, cap_in, heat, shift, g_img, g_txt, means,
    pic, cap, images, texts, sims, scaled, scaled_t, img_term, img_send, txt_send, txt_own,
    from_x, to_y, from_y, from_y4, from_c, to_z, from_z, to_far, part, sum_in,
    s_in, s_gather, r_gather, s_scatter, r_scatter, s_sum, r_sum,
):
    img, txt = lax.axis_index("img"), lax.axis_index("txt")
    x, y, c = img // 2, txt // 12, txt % 2
    z = (img % 2) * 6 + (txt // 2) % 6

    def at(dx=0, dy=0, dz=0, dc=0):
        zz = (z + dz) % NZ
        return (((x + dx) % NX) * 2 + zz // 6, (((y + dy) % NY) * 6 + zz % 6) * 2 + (c + dc) % 2)

    peers = [at(dy=d) for d in (4, 3, 5, 2, 6, 1, 7)] + [at(dx=d) for d in DX]
    peers += [at(dz=d) for d in (4, 8, 3, 9, 2, 10, 1, 11)] + [at(dc=1)]
    entry = pltpu.get_barrier_semaphore()
    for peer in peers:
        pl.semaphore_signal(entry, inc=1, device_id=peer, device_id_type=MESH)
    loads = [pltpu.make_async_copy(pic_in, pic, s_in.at[0]), pltpu.make_async_copy(cap_in, cap, s_in.at[1])]
    for load in loads:
        load.start()
    for load in loads:
        load.wait()

    def normalize(ref):
        values = ref[...].astype(jnp.float32)
        norm = jnp.sqrt(jnp.sum(values * values, axis=1, keepdims=True) + EPS)
        return values / norm, norm

    img_unit, img_norm = normalize(pic)
    txt_unit, txt_norm = normalize(cap)
    images[0:B, :] = img_unit.astype(jnp.bfloat16)
    texts[0:B, :] = txt_unit.astype(jnp.bfloat16)
    pl.semaphore_wait(entry, len(peers))

    sends = []

    def sender(ssem, rsem):
        used = [0]

        def send(src, dst, device):
            i = used[0]
            used[0] += 1
            copy = pltpu.make_async_remote_copy(
                src_ref=src, dst_ref=dst, send_sem=ssem.at[i], recv_sem=rsem.at[i],
                device_id=device, device_id_type=MESH)
            copy.start()
            sends.append(copy)
            return copy

        return send

    def slots(ref, first, count=1):
        return ref.at[pl.ds(first * B, count * B)]

    def wait(copies):
        for copy in copies:
            copy.wait_recv()

    send = sender(s_gather, r_gather)
    own_t, own_i = slots(texts, 0), slots(images, 0)
    over_z = {d: send(own_t, slots(texts, SLOT[d]), at(dz=-d)) for d in (4, 8)}
    over_y = {k: send(own_i, slots(images, 4 * k), at(dy=-DY[k])) for k in range(1, 7)}
    over_x, over_c = {}, []

    def forward_x(*ks):
        for k in ks:
            if k:
                over_y[k].wait_recv()
            over_x[k] = [send(slots(images, 4 * k), slots(images, 4 * k + dx), at(dx=-dx)) for dx in DX]

    def forward_c(*ds):
        first = min(SLOT[d] for d in ds)
        over_c.append(send(slots(texts, first, len(ds)), slots(texts, NZ + first, len(ds)), at(dc=1)))

    forward_x(0)
    forward_c(0)
    forward_x(1, 2)
    for d in (3, 9, 2, 10, 1, 11):
        over_z[d] = send(own_t, slots(texts, SLOT[d]), at(dz=-d))
    wait(over_x[0])
    over_x[7] = [send(slots(images, 0, 4), slots(images, 28, 4), at(dy=-4))]
    wait([over_z[4], over_z[8]])
    six = SLOT[6] * B
    late = [
        send(texts.at[pl.ds(SLOT[4] * B, B), pl.ds(0, HALF)], texts.at[pl.ds(six, B), pl.ds(0, HALF)], at(dz=-2)),
        send(texts.at[pl.ds(SLOT[8] * B, B), pl.ds(HALF, HALF)], texts.at[pl.ds(six, B), pl.ds(HALF, HALF)], at(dz=2)),
        send(slots(texts, SLOT[4]), slots(texts, SLOT[5]), at(dz=-1)),
        send(slots(texts, SLOT[8]), slots(texts, SLOT[7]), at(dz=1)),
    ]
    forward_x(3, 4)
    forward_c(4, 8)
    wait([over_z[d] for d in (1, 11, 2, 10)])
    forward_c(1, 11, 2, 10)
    forward_x(5, 6)
    wait([over_z[d] for d in (3, 9)])
    forward_c(3, 9)
    wait(late)
    forward_c(5, 7, 6)

    def owner_offset(k, n):
        return jnp.where((k & 1) == 1, (k + 1) >> 1, jnp.where(k == 0, 0, n - (k >> 1)))

    col = lax.broadcasted_iota(jnp.int32, (1, TXT), 1)
    k = col >> 4
    dc = jnp.where(k >= NZ, 1, 0)
    zz = z + owner_offset(k - NZ * dc, NZ)
    zz = jnp.where(zz >= NZ, zz - NZ, zz)
    z_hi = jnp.where(zz >= 6, 1, 0)
    cc = c + dc - 2 * c * dc
    txt_id = (((y * 6 + zz - 6 * z_hi) * 2 + cc) * 8 + x * 2 + z_hi) * B + (col & (B - 1))
    temp = jnp.exp(jnp.full((1, TXT), heat[0], jnp.float32))
    bias = shift[0]
    step = 32

    def pairs(i, sums):
        first = pl.multiple_of(i * step, step)
        sim = sims[pl.ds(first, step), :]
        r = lax.broadcasted_iota(jnp.int32, (step, 1), 0) + first
        xo = (x + (r >> 4)) & (NX - 1)
        yo = (y + owner_offset(r >> 6, NY)) & (NY - 1)
        img_id = ((xo * 2 + z // 6) * 96 + (yo * 6 + z % 6) * 2 + c) * B + (r & (B - 1))
        same = img_id == txt_id
        logits = temp * sim + bias
        arg = jnp.where(same, -logits, logits)
        e = jnp.exp(-jnp.abs(arg))
        loss = jnp.maximum(arg, 0.0) + jnp.log1p(e)
        sig = jnp.where(arg >= 0, 1.0, e) / (1.0 + e)
        coeff = jnp.where(same, -sig, sig)
        scaled[pl.ds(first, step), :] = (temp * coeff).astype(jnp.bfloat16)

        def fold(v):
            return jnp.sum(v.reshape(step // 8, 8, TXT), axis=0)

        return sums[0] + fold(loss), sums[1] + fold(coeff), sums[2] + fold(coeff * sim)

    zero = jnp.zeros((8, TXT), jnp.float32)
    sums = (zero, zero, zero)
    send = sender(s_scatter, r_scatter)
    nt = (((1,), (1,)), ((), ()))
    back_x = {}
    wait(over_c)
    for p, (a, b) in enumerate(PARTS):
        ks = (range(0, 5), range(5, 8))[p]
        for k in ks:
            if k:
                wait(over_x[k])
        sims[a:b, :] = lax.dot_general(images[a:b, :], texts[...], nt, preferred_element_type=jnp.float32)
        sums = lax.fori_loop(a // step, b // step, pairs, sums)
        if p:
            def whole(v):
                v = v[:, 0:128] + v[:, 128:256] + v[:, 256:384]
                return jnp.sum(jnp.sum(v, axis=0, keepdims=True), axis=1, keepdims=True)

            lane = lax.broadcasted_iota(jnp.int32, (1, 128), 1)
            total = jnp.where(lane == 0, whole(sums[0]), jnp.where(lane == 1, whole(sums[1]), whole(sums[2])))
            send_sum = sender(s_sum, r_sum)
            used = [0]

            def spread(stage, value, devices):
                part[stage] = value
                copies = []
                for device in devices:
                    copies.append((send_sum(part.at[stage], sum_in.at[used[0]], device), used[0]))
                    used[0] += 1
                return copies

            def collect(value, copies):
                for copy, i in copies:
                    copy.wait_recv()
                    value = value + sum_in[i]
                return value

            plane = [at(dx, dy) for dy in DY[::-1] for dx in (2, 1, 3, 0) if dx or dy]
            sum_p = spread(0, total, plane)
            scaled_t[...] = scaled[...].T
            txt_send[...] = jnp.dot(scaled_t[CR:, :], images[...], preferred_element_type=jnp.float32).astype(jnp.bfloat16)
            cut = SLOT[4]
            back_c = [send(slots(txt_send, i, n), slots(from_c, i, n), at(dc=1)) for i, n in ((cut, NZ - cut), (0, cut))]
            txt_own[...] = jnp.dot(scaled_t[0:CR, :], images[...], preferred_element_type=jnp.float32)
        term = jnp.dot(scaled[a:b, :], texts[...], preferred_element_type=jnp.float32)
        img_term[a:b, :] = term
        img_send[a:b, :] = term.astype(jnp.bfloat16)
    def send_x(*ks):
        for k in ks:
            back_x[k] = [send(slots(img_send, 4 * k + dx), slots(from_x, 4 * k + dx), at(dx=dx)) for dx in DX]

    back_y4 = send(slots(img_send, 28, 4), from_y4, at(dy=4))
    send_x(6, 5, 4, 3, 2, 1)

    def add_c(first, last):
        value = txt_own[first * B:last * B, :] + from_c[first * B:last * B, :].astype(jnp.float32)
        txt_own[first * B:last * B, :] = value
        to_z[first * B:last * B, :] = value.astype(jnp.bfloat16)

    back_c[0].wait_recv()
    add_c(cut, NZ)
    relay = [
        send(to_z.at[pl.ds(six, B), pl.ds(0, HALF)], from_z.at[pl.ds(six, B), pl.ds(0, HALF)], at(dz=2)),
        send(to_z.at[pl.ds(six, B), pl.ds(HALF, HALF)], from_z.at[pl.ds(six, B), pl.ds(HALF, HALF)], at(dz=-2)),
        send(slots(to_z, SLOT[5]), slots(from_z, SLOT[5]), at(dz=1)),
        send(slots(to_z, SLOT[7]), slots(from_z, SLOT[7]), at(dz=-1)),
    ]
    back_c[1].wait_recv()
    add_c(0, cut)
    back_z = {}

    def send_z(*ds):
        for d in ds:
            back_z[d] = send(slots(to_z, SLOT[d]), slots(from_z, SLOT[d]), at(dz=d))

    send_z(2, 10, 1, 11)

    total = collect(total, sum_p)
    column = [at(dz=d, dc=other) for d in DZ[::-1] for other in (0, 1) if d or other]
    sum_z = spread(1, total, column)
    wait(relay)

    def piece(ref, d):
        return ref[SLOT[d] * B:(SLOT[d] + 1) * B, :].astype(jnp.float32)

    side = lax.broadcasted_iota(jnp.int32, (B, E), 1) < HALF
    both = piece(from_z, 6)
    to_far[0:B, :] = (piece(txt_own, 4) + piece(from_z, 5) + jnp.where(side, both, 0.0)).astype(jnp.bfloat16)
    to_far[B:, :] = (piece(txt_own, 8) + piece(from_z, 7) + jnp.where(side, 0.0, both)).astype(jnp.bfloat16)
    for i, d in enumerate((4, 8)):
        back_z[d] = send(slots(to_far, i), slots(from_z, SLOT[d]), at(dz=d))
    send_z(3, 9)
    back_y4.wait_recv()
    near_y = img_term[0:4 * B, :] + from_y4[...].astype(jnp.float32)
    img_term[0:4 * B, :] = near_y
    img_send[0:4 * B, :] = near_y.astype(jnp.bfloat16)
    send_x(0)
    back_y = []

    def image_sum(k):
        wait(back_x[k])
        first = 4 * k * B
        value = img_term[first:first + B, :]
        for dx in (1, 2, 3):
            value = value + from_x[first + dx * B:first + (dx + 1) * B, :].astype(jnp.float32)
        return value

    def send_y(*ks):
        for k in ks:
            to_y[(k - 1) * B:k * B, :] = image_sum(k).astype(jnp.bfloat16)
            back_y.append(send(slots(to_y, k - 1), slots(from_y, k - 1), at(dy=DY[k])))

    send_y(6, 5, 4, 3, 2, 1)
    img_dir = image_sum(0)

    def back_norm(unit, direction, norm):
        inner = jnp.sum(unit * direction, axis=1, keepdims=True)
        return (direction - unit * inner) / norm

    txt_dir = piece(txt_own, 0)
    for d in (1, 11, 2, 10, 3, 9, 4, 8):
        back_z[d].wait_recv()
        txt_dir = txt_dir + piece(from_z, d)
    g_txt[...] = back_norm(txt_unit, txt_dir, txt_norm)
    wait(back_y)
    for k in range(1, 7):
        img_dir = img_dir + from_y[(k - 1) * B:k * B, :].astype(jnp.float32)
    g_img[...] = back_norm(img_unit, img_dir, img_norm)
    total = collect(total, sum_z)
    means[...] = total * jnp.where(lane == 2, temp[:, 0:128], 1.0) * (1.0 / (COUNT * COUNT))
    for copy in sends:
        copy.wait_send()


def hand_over(a, b, c, a_out, b_out, c_out):
    a_out[...] = a[...]
    b_out[...] = b[...]
    for i in range(3):
        c_out[i] = jnp.sum(c[:, i:i + 1])


def per_device(pictures, captions, heat, shift):
    f32, bf16 = jnp.float32, jnp.bfloat16
    hbm, vmem, smem = (pl.BlockSpec(memory_space=m) for m in (pltpu.HBM, pltpu.VMEM, pltpu.SMEM))
    dma = pltpu.SemaphoreType.DMA
    results_shape = (
        jax.ShapeDtypeStruct((B, E), f32),
        jax.ShapeDtypeStruct((B, E), f32),
        jax.ShapeDtypeStruct((1, 128), f32),
    )
    results = pl.pallas_call(
        kernel,
        out_shape=results_shape,
        in_specs=[hbm, hbm, smem, smem],
        out_specs=(vmem, vmem, vmem),
        scratch_shapes=[
            pltpu.VMEM((B, E), bf16),
            pltpu.VMEM((B, E), bf16),
            pltpu.VMEM((IMG, E), bf16),
            pltpu.VMEM((TXT, E), bf16),
            pltpu.VMEM((IMG, TXT), f32),
            pltpu.VMEM((IMG, TXT), bf16),
            pltpu.VMEM((TXT, IMG), bf16),
            pltpu.VMEM((IMG, E), f32),
            pltpu.VMEM((IMG, E), bf16),
            pltpu.VMEM((CR, E), bf16),
            pltpu.VMEM((CR, E), f32),
            pltpu.VMEM((IMG, E), bf16),
            pltpu.VMEM((7 * B, E), bf16),
            pltpu.VMEM((7 * B, E), bf16),
            pltpu.VMEM((4 * B, E), bf16),
            pltpu.VMEM((CR, E), bf16),
            pltpu.VMEM((CR, E), bf16),
            pltpu.VMEM((CR, E), bf16),
            pltpu.VMEM((2 * B, E), bf16),
            pltpu.VMEM((2, 1, 128), f32),
            pltpu.VMEM((54, 1, 128), f32),
            dma((2,)), dma((48,)), dma((48,)), dma((44,)), dma((44,)), dma((54,)), dma((54,)),
        ],
        compiler_params=pltpu.CompilerParams(
            collective_id=0, has_side_effects=True, vmem_limit_bytes=62 * 1024 * 1024),
        cost_estimate=pl.CostEstimate(flops=910_000_000, bytes_accessed=150_000, transcendentals=600_000),
        name="pairs",
    )(pictures, captions, heat.reshape(1), shift.reshape(1))
    return pl.pallas_call(
        hand_over,
        out_shape=(*results_shape[:2], jax.ShapeDtypeStruct((3,), f32)),
        in_specs=[vmem] * 3,
        out_specs=(vmem, vmem, smem),
        compiler_params=pltpu.CompilerParams(vmem_limit_bytes=62 * 1024 * 1024),
        name="hand_over",
    )(*results)


def solution(mesh):
    in_specs = (P(("img", "txt"), None), P(("txt", "img"), None), P(), P())
    out_specs = (P(("img", "txt"), None), P(("txt", "img"), None), P())
    return jax.shard_map(
        per_device, mesh=mesh, in_specs=in_specs, out_specs=out_specs, check_vma=False
    )
```

```python
import jax
import jax.numpy as jnp
from jax import lax
from jax.experimental import pallas as pl
from jax.experimental.pallas import tpu as pltpu
from jax.sharding import PartitionSpec as P

MESH = pl.DeviceIdType.MESH
NX, NY, NZ = 4, 8, 12
B, E = 16, 768
EPS = 1e-6
COUNT = 12288.0
HALF = E // 2

DY = (0, 1, 7, 2, 6, 3, 5, 4)
DZ = (0, 1, 11, 2, 10, 3, 9, 4, 8, 5, 7, 6)
SLOT = {d: k for k, d in enumerate(DZ)}
IMG, TXT = NX * NY * B, NZ * 2 * B
CR = NZ * B
FIRST = 5 * NX * B
PARTS = ((0, FIRST), (FIRST, IMG))
DX = (2, 1, 3)


def kernel(
    pic_in, cap_in, heat, shift, g_img, g_txt, means,
    pic, cap, images, texts, sims, scaled, scaled_t, img_term, img_send, txt_send, txt_own,
    from_x, to_y, from_y, from_y4, from_c, to_z, from_z, to_far, part, sum_in,
    s_in, s_gather, r_gather, s_scatter, r_scatter, s_sum, r_sum,
):
    img, txt = lax.axis_index("img"), lax.axis_index("txt")
    x, y, c = img // 2, txt // 12, txt % 2
    z = (img % 2) * 6 + (txt // 2) % 6

    def at(dx=0, dy=0, dz=0, dc=0):
        zz = (z + dz) % NZ
        return (((x + dx) % NX) * 2 + zz // 6, (((y + dy) % NY) * 6 + zz % 6) * 2 + (c + dc) % 2)

    peers = [at(dy=d) for d in (4, 3, 5, 2, 6, 1, 7)] + [at(dx=d) for d in DX]
    peers += [at(dz=d) for d in (4, 8, 3, 9, 2, 10, 1, 11)] + [at(dc=1)]
    entry = pltpu.get_barrier_semaphore()
    for peer in peers:
        pl.semaphore_signal(entry, inc=1, device_id=peer, device_id_type=MESH)
    loads = [pltpu.make_async_copy(pic_in, pic, s_in.at[0]), pltpu.make_async_copy(cap_in, cap, s_in.at[1])]
    for load in loads:
        load.start()
    for load in loads:
        load.wait()

    def normalize(ref):
        values = ref[...].astype(jnp.float32)
        norm = jnp.sqrt(jnp.sum(values * values, axis=1, keepdims=True) + EPS)
        return values / norm, norm

    img_unit, img_norm = normalize(pic)
    txt_unit, txt_norm = normalize(cap)
    images[0:B, :] = img_unit.astype(jnp.bfloat16)
    texts[0:B, :] = txt_unit.astype(jnp.bfloat16)
    pl.semaphore_wait(entry, len(peers))

    sends = []

    def sender(ssem, rsem):
        used = [0]

        def send(src, dst, device):
            i = used[0]
            used[0] += 1
            copy = pltpu.make_async_remote_copy(
                src_ref=src, dst_ref=dst, send_sem=ssem.at[i], recv_sem=rsem.at[i],
                device_id=device, device_id_type=MESH)
            copy.start()
            sends.append(copy)
            return copy

        return send

    def slots(ref, first, count=1):
        return ref.at[pl.ds(first * B, count * B)]

    def wait(copies):
        for copy in copies:
            copy.wait_recv()

    send = sender(s_gather, r_gather)
    own_t, own_i = slots(texts, 0), slots(images, 0)
    over_z = {d: send(own_t, slots(texts, SLOT[d]), at(dz=-d)) for d in (4, 8)}
    over_y = {k: send(own_i, slots(images, 4 * k), at(dy=-DY[k])) for k in range(1, 7)}
    over_x, over_c = {}, []

    def forward_x(*ks):
        for k in ks:
            if k:
                over_y[k].wait_recv()
            over_x[k] = [send(slots(images, 4 * k), slots(images, 4 * k + dx), at(dx=-dx)) for dx in DX]

    def forward_c(*ds):
        first = min(SLOT[d] for d in ds)
        over_c.append(send(slots(texts, first, len(ds)), slots(texts, NZ + first, len(ds)), at(dc=1)))

    forward_x(0)
    forward_c(0)
    forward_x(1, 2)
    for d in (3, 9, 2, 10, 1, 11):
        over_z[d] = send(own_t, slots(texts, SLOT[d]), at(dz=-d))
    wait(over_x[0])
    over_x[7] = [send(slots(images, 0, 4), slots(images, 28, 4), at(dy=-4))]
    wait([over_z[4], over_z[8]])
    six = SLOT[6] * B
    late = [
        send(texts.at[pl.ds(SLOT[4] * B, B), pl.ds(0, HALF)], texts.at[pl.ds(six, B), pl.ds(0, HALF)], at(dz=-2)),
        send(texts.at[pl.ds(SLOT[8] * B, B), pl.ds(HALF, HALF)], texts.at[pl.ds(six, B), pl.ds(HALF, HALF)], at(dz=2)),
        send(slots(texts, SLOT[4]), slots(texts, SLOT[5]), at(dz=-1)),
        send(slots(texts, SLOT[8]), slots(texts, SLOT[7]), at(dz=1)),
    ]
    forward_x(3, 4)
    forward_c(4, 8)
    wait([over_z[d] for d in (1, 11, 2, 10)])
    forward_c(1, 11, 2, 10)
    forward_x(5, 6)
    wait([over_z[d] for d in (3, 9)])
    forward_c(3, 9)
    wait(late)
    forward_c(5, 7, 6)

    def owner_offset(k, n):
        return jnp.where((k & 1) == 1, (k + 1) >> 1, jnp.where(k == 0, 0, n - (k >> 1)))

    col = lax.broadcasted_iota(jnp.int32, (1, TXT), 1)
    k = col >> 4
    dc = jnp.where(k >= NZ, 1, 0)
    zz = z + owner_offset(k - NZ * dc, NZ)
    zz = jnp.where(zz >= NZ, zz - NZ, zz)
    z_hi = jnp.where(zz >= 6, 1, 0)
    cc = c + dc - 2 * c * dc
    txt_id = (((y * 6 + zz - 6 * z_hi) * 2 + cc) * 8 + x * 2 + z_hi) * B + (col & (B - 1))
    temp = jnp.exp(jnp.full((1, TXT), heat[0], jnp.float32))
    bias = shift[0]
    step = 32

    def pairs(i, sums):
        first = pl.multiple_of(i * step, step)
        sim = sims[pl.ds(first, step), :]
        r = lax.broadcasted_iota(jnp.int32, (step, 1), 0) + first
        xo = (x + (r >> 4)) & (NX - 1)
        yo = (y + owner_offset(r >> 6, NY)) & (NY - 1)
        img_id = ((xo * 2 + z // 6) * 96 + (yo * 6 + z % 6) * 2 + c) * B + (r & (B - 1))
        same = img_id == txt_id
        logits = temp * sim + bias
        arg = jnp.where(same, -logits, logits)
        e = jnp.exp(-jnp.abs(arg))
        loss = jnp.maximum(arg, 0.0) + jnp.log1p(e)
        sig = jnp.where(arg >= 0, 1.0, e) / (1.0 + e)
        coeff = jnp.where(same, -sig, sig)
        scaled[pl.ds(first, step), :] = (temp * coeff).astype(jnp.bfloat16)

        def fold(v):
            return jnp.sum(v.reshape(step // 8, 8, TXT), axis=0)

        return sums[0] + fold(loss), sums[1] + fold(coeff), sums[2] + fold(coeff * sim)

    zero = jnp.zeros((8, TXT), jnp.float32)
    sums = (zero, zero, zero)
    send = sender(s_scatter, r_scatter)
    nt = (((1,), (1,)), ((), ()))
    back_x = {}
    wait(over_c)
    for p, (a, b) in enumerate(PARTS):
        ks = (range(0, 5), range(5, 8))[p]
        for k in ks:
            if k:
                wait(over_x[k])
        sims[a:b, :] = lax.dot_general(images[a:b, :], texts[...], nt, preferred_element_type=jnp.float32)
        sums = lax.fori_loop(a // step, b // step, pairs, sums)
        if p:
            def whole(v):
                v = v[:, 0:128] + v[:, 128:256] + v[:, 256:384]
                return jnp.sum(jnp.sum(v, axis=0, keepdims=True), axis=1, keepdims=True)

            lane = lax.broadcasted_iota(jnp.int32, (1, 128), 1)
            total = jnp.where(lane == 0, whole(sums[0]), jnp.where(lane == 1, whole(sums[1]), whole(sums[2])))
            send_sum = sender(s_sum, r_sum)
            used = [0]

            def spread(stage, value, devices):
                part[stage] = value
                copies = []
                for device in devices:
                    copies.append((send_sum(part.at[stage], sum_in.at[used[0]], device), used[0]))
                    used[0] += 1
                return copies

            def collect(value, copies):
                for copy, i in copies:
                    copy.wait_recv()
                    value = value + sum_in[i]
                return value

            plane = [at(dx, dy) for dy in DY[::-1] for dx in (2, 1, 3, 0) if dx or dy]
            sum_p = spread(0, total, plane)
            scaled_t[...] = scaled[...].T
            txt_send[...] = jnp.dot(scaled_t[CR:, :], images[...], preferred_element_type=jnp.float32).astype(jnp.bfloat16)
            cut = SLOT[4]
            back_c = [send(slots(txt_send, i, n), slots(from_c, i, n), at(dc=1)) for i, n in ((cut, NZ - cut), (0, cut))]
            txt_own[...] = jnp.dot(scaled_t[0:CR, :], images[...], preferred_element_type=jnp.float32)
        term = jnp.dot(scaled[a:b, :], texts[...], preferred_element_type=jnp.float32)
        img_term[a:b, :] = term
        img_send[a:b, :] = term.astype(jnp.bfloat16)
    def send_x(*ks):
        for k in ks:
            back_x[k] = [send(slots(img_send, 4 * k + dx), slots(from_x, 4 * k + dx), at(dx=dx)) for dx in DX]

    back_y4 = send(slots(img_send, 28, 4), from_y4, at(dy=4))
    send_x(6, 5, 4)

    def add_c(first, last):
        value = txt_own[first * B:last * B, :] + from_c[first * B:last * B, :].astype(jnp.float32)
        txt_own[first * B:last * B, :] = value
        to_z[first * B:last * B, :] = value.astype(jnp.bfloat16)

    back_c[0].wait_recv()
    add_c(cut, NZ)
    relay = [
        send(to_z.at[pl.ds(six, B), pl.ds(0, HALF)], from_z.at[pl.ds(six, B), pl.ds(0, HALF)], at(dz=2)),
        send(to_z.at[pl.ds(six, B), pl.ds(HALF, HALF)], from_z.at[pl.ds(six, B), pl.ds(HALF, HALF)], at(dz=-2)),
        send(slots(to_z, SLOT[5]), slots(from_z, SLOT[5]), at(dz=1)),
        send(slots(to_z, SLOT[7]), slots(from_z, SLOT[7]), at(dz=-1)),
    ]
    back_c[1].wait_recv()
    add_c(0, cut)
    back_z = {}

    def send_z(*ds):
        for d in ds:
            back_z[d] = send(slots(to_z, SLOT[d]), slots(from_z, SLOT[d]), at(dz=d))

    send_z(2, 10, 1, 11)
    send_x(3, 2, 1)

    total = collect(total, sum_p)
    column = [at(dz=d, dc=other) for d in DZ[::-1] for other in (0, 1) if d or other]
    sum_z = spread(1, total, column)
    wait(relay)

    def piece(ref, d):
        return ref[SLOT[d] * B:(SLOT[d] + 1) * B, :].astype(jnp.float32)

    side = lax.broadcasted_iota(jnp.int32, (B, E), 1) < HALF
    both = piece(from_z, 6)
    to_far[0:B, :] = (piece(txt_own, 4) + piece(from_z, 5) + jnp.where(side, both, 0.0)).astype(jnp.bfloat16)
    to_far[B:, :] = (piece(txt_own, 8) + piece(from_z, 7) + jnp.where(side, 0.0, both)).astype(jnp.bfloat16)
    for i, d in enumerate((4, 8)):
        back_z[d] = send(slots(to_far, i), slots(from_z, SLOT[d]), at(dz=d))
    send_z(3, 9)
    back_y4.wait_recv()
    near_y = img_term[0:4 * B, :] + from_y4[...].astype(jnp.float32)
    img_term[0:4 * B, :] = near_y
    img_send[0:4 * B, :] = near_y.astype(jnp.bfloat16)
    send_x(0)
    back_y = []

    def image_sum(k):
        wait(back_x[k])
        first = 4 * k * B
        value = img_term[first:first + B, :]
        for dx in (1, 2, 3):
            value = value + from_x[first + dx * B:first + (dx + 1) * B, :].astype(jnp.float32)
        return value

    def send_y(*ks):
        for k in ks:
            to_y[(k - 1) * B:k * B, :] = image_sum(k).astype(jnp.bfloat16)
            back_y.append(send(slots(to_y, k - 1), slots(from_y, k - 1), at(dy=DY[k])))

    send_y(6, 5, 4, 3, 2, 1)
    img_dir = image_sum(0)

    def back_norm(unit, direction, norm):
        inner = jnp.sum(unit * direction, axis=1, keepdims=True)
        return (direction - unit * inner) / norm

    txt_dir = piece(txt_own, 0)
    for d in (1, 11, 2, 10, 3, 9, 4, 8):
        back_z[d].wait_recv()
        txt_dir = txt_dir + piece(from_z, d)
    g_txt[...] = back_norm(txt_unit, txt_dir, txt_norm)
    wait(back_y)
    for k in range(1, 7):
        img_dir = img_dir + from_y[(k - 1) * B:k * B, :].astype(jnp.float32)
    g_img[...] = back_norm(img_unit, img_dir, img_norm)
    total = collect(total, sum_z)
    means[...] = total * jnp.where(lane == 2, temp[:, 0:128], 1.0) * (1.0 / (COUNT * COUNT))
    for copy in sends:
        copy.wait_send()


def hand_over(a, b, c, a_out, b_out, c_out):
    a_out[...] = a[...]
    b_out[...] = b[...]
    for i in range(3):
        c_out[i] = jnp.sum(c[:, i:i + 1])


def per_device(pictures, captions, heat, shift):
    f32, bf16 = jnp.float32, jnp.bfloat16
    hbm, vmem, smem = (pl.BlockSpec(memory_space=m) for m in (pltpu.HBM, pltpu.VMEM, pltpu.SMEM))
    dma = pltpu.SemaphoreType.DMA
    results_shape = (
        jax.ShapeDtypeStruct((B, E), f32),
        jax.ShapeDtypeStruct((B, E), f32),
        jax.ShapeDtypeStruct((1, 128), f32),
    )
    results = pl.pallas_call(
        kernel,
        out_shape=results_shape,
        in_specs=[hbm, hbm, smem, smem],
        out_specs=(vmem, vmem, vmem),
        scratch_shapes=[
            pltpu.VMEM((B, E), bf16),
            pltpu.VMEM((B, E), bf16),
            pltpu.VMEM((IMG, E), bf16),
            pltpu.VMEM((TXT, E), bf16),
            pltpu.VMEM((IMG, TXT), f32),
            pltpu.VMEM((IMG, TXT), bf16),
            pltpu.VMEM((TXT, IMG), bf16),
            pltpu.VMEM((IMG, E), f32),
            pltpu.VMEM((IMG, E), bf16),
            pltpu.VMEM((CR, E), bf16),
            pltpu.VMEM((CR, E), f32),
            pltpu.VMEM((IMG, E), bf16),
            pltpu.VMEM((7 * B, E), bf16),
            pltpu.VMEM((7 * B, E), bf16),
            pltpu.VMEM((4 * B, E), bf16),
            pltpu.VMEM((CR, E), bf16),
            pltpu.VMEM((CR, E), bf16),
            pltpu.VMEM((CR, E), bf16),
            pltpu.VMEM((2 * B, E), bf16),
            pltpu.VMEM((2, 1, 128), f32),
            pltpu.VMEM((54, 1, 128), f32),
            dma((2,)), dma((48,)), dma((48,)), dma((44,)), dma((44,)), dma((54,)), dma((54,)),
        ],
        compiler_params=pltpu.CompilerParams(
            collective_id=0, has_side_effects=True, vmem_limit_bytes=62 * 1024 * 1024),
        cost_estimate=pl.CostEstimate(flops=910_000_000, bytes_accessed=150_000, transcendentals=600_000),
        name="pairs",
    )(pictures, captions, heat.reshape(1), shift.reshape(1))
    return pl.pallas_call(
        hand_over,
        out_shape=(*results_shape[:2], jax.ShapeDtypeStruct((3,), f32)),
        in_specs=[vmem] * 3,
        out_specs=(vmem, vmem, smem),
        compiler_params=pltpu.CompilerParams(vmem_limit_bytes=62 * 1024 * 1024),
        name="hand_over",
    )(*results)


def solution(mesh):
    in_specs = (P(("img", "txt"), None), P(("txt", "img"), None), P(), P())
    out_specs = (P(("img", "txt"), None), P(("txt", "img"), None), P())
    return jax.shard_map(
        per_device, mesh=mesh, in_specs=in_specs, out_specs=out_specs, check_vma=False
    )
```
